32 devices in a mesh: rep: 1, ep: 8 (over z, y), dp: 2 (over x), sp: 2 (over core).
Axes of the slice: x: 2, y: 2, z: 4, core: 2. Of those that a mesh axis runs over, the one named last changes fastest.
Arguments:
- hidden_states: bfloat16 [2048, 4096], P(('rep', 'ep', 'sp'), 'dp'), may hold values from -6 to 6
- norm_gain: bfloat16 [4096], P('dp'), may hold values from 0.099609375 to 1.8984375
- up_proj: bfloat16 [16, 4096, 768], P(('ep', 'sp'), 'dp'), may hold values from -0.09375 to 0.09375
- down_proj: bfloat16 [16, 768, 4096], P(('ep', 'sp'), None, 'dp'), may hold values from -0.21875 to 0.21875
- expert_ids: int32 [2048, 8], P(('rep', 'ep', 'sp')), may hold values from 0 to 15, all different within a row; in each aligned block of 128 rows (0 to 127, 128 to 255, ...) at most 80 rows name the same one
- combine_num: int32 [2048, 8], P(('rep', 'ep', 'sp')), may hold values from 2048 to 65535
Outputs:
- mixed: bfloat16 [2048, 4096], P(('rep', 'ep', 'sp'), 'dp')
The draws below stay inside these ranges and needn't reach their ends.
Inputs may be any that keep to these rules, and one draw needn't show every extreme that they name: `expert_ids`: each row names 8 different experts; among the 128 rows that one device holds (an aligned block) no expert is named more than 80 times, a bound that some block reaches.
All inputs are finite; a program needn't handle non-finite values.
Results may differ from the reference program's by a relative error of at most 0.008.
Values may be sent and summed in bfloat16 or wider, within the bound.
A program may use at most 64 MiB of HBM per device.

```python
import math
import jax
import jax.numpy as jnp
import numpy as np
from jax import lax

D = 4096
FFH = 768
TOPK = 8
TOK_DEV = 128
EXPERTS = 16
CAP = 80
TOKENS = 2048


def with_ends(values, own_key, smallest, top_value):
    longest = values.shape.index(max(values.shape))
    spots = []
    for shift in (0, 1):
        where = [jax.random.randint(jax.random.fold_in(own_key, axis), (), 0, length) for axis, length in enumerate(values.shape)]
        where[longest] = (where[longest] + shift) % values.shape[longest]
        spots.append(tuple(where))
    return values.at[spots[0]].set(smallest).at[spots[1]].set(top_value)


def shard_levels(stream_key, dims, shards, least, high):
    def one(axis_at, parts):
        draws = jax.random.uniform(jax.random.fold_in(jax.random.fold_in(stream_key, 6), axis_at), (parts,), jnp.float32, least / len(shards), high / len(shards))
        return jnp.repeat(jnp.exp(draws), dims[axis_at] // parts).reshape((-1,) + (1,) * (len(dims) - axis_at - 1))

    gain = one(*shards[0])
    for cut in shards[1:]:
        gain = gain * one(*cut)
    return gain


def deal_out(stream_key, own, number, rows, amount, top, most, lean):
    order = jax.random.permutation(stream_key, amount)
    packed, ordinary = load_shares(amount, rows * top, most, lean, True), load_shares(amount, rows * top, most, lean, False)
    places = jnp.arange(amount)

    def named(tallies, offset_by):
        used = int((tallies > 0).sum())
        fixed = max(1, used // 4)
        passed = fixed + (places - fixed + offset_by * (used - fixed)) % max(1, amount - fixed)
        return jnp.zeros((amount,), jnp.int32).at[order[jnp.where(places < fixed, places, passed)]].set(jnp.asarray(tallies, jnp.int32))

    tallies = jnp.where(number % 4 == 0, named(packed, number // 4), named(ordinary, number - number // 4 - 1))
    mixed = jax.random.permutation(jax.random.fold_in(own, 3), amount)
    giver, sink = mixed[0:amount // 2 * 2:2], mixed[1:amount // 2 * 2:2]
    room = jnp.minimum(tallies[giver] - 1, most - tallies[sink]) // 2
    room = jnp.where((giver == order[0]) | (sink == order[0]) | (tallies[sink] == 0), 0, jnp.maximum(room, 0))
    passed = jax.random.randint(jax.random.fold_in(own, 4), (amount // 2,), 0, 1 << 20) % (room + 1)
    tallies = tallies.at[giver].add(-passed).at[sink].add(passed)
    labels = jnp.searchsorted(jnp.cumsum(tallies), jnp.arange(rows * top), side="right").astype(jnp.int32)
    grid = labels.reshape(top, rows).T
    grid = grid[jax.random.permutation(jax.random.fold_in(own, 1), rows)]
    offset_by = jax.random.randint(jax.random.fold_in(own, 2), (rows, 1), 0, top)
    return jnp.take_along_axis(grid, (jnp.arange(top)[None, :] + offset_by) % top, axis=1)


def load_shares(count, total, reach, slope, full):
    loads = [(1 << 20) // math.isqrt(standing ** slope) + 1 for standing in range(1, count + 1)]
    largest = reach if full else min(reach, max(-(-total // count), total * loads[0] // sum(loads)))
    least = 1 if total - largest >= count - 1 else 0
    given, spare = [largest] + [least] * (count - 1), total - largest - least * (count - 1)
    while spare > 0:
        candidates = [i for i in range(1, count) if given[i] < largest] or [i for i in range(1, count) if given[i] < reach]
        pool, budget = sum([loads[i] for i in candidates]), spare
        for i in candidates:
            extra = min(reach - given[i], max(1, budget * loads[i] // pool), spare)
            given[i] = given[i] + extra
            spare = spare - extra
    return np.array(given)


def centred(rng, shape, deviation, reach, cuts=(), kind=jnp.bfloat16):
    result = deviation * jax.random.normal(rng, shape, jnp.float32)
    if cuts:
        result = result * shard_levels(rng, shape, cuts, -0.22, 0.18)
    return jnp.clip(result, -reach, reach).astype(kind)


def setup_inputs(seed: int = 0, part: int = 0) -> dict:
    splits = jax.random.split(jax.random.key(seed), 7)
    part_keys = jax.random.split(jax.random.fold_in(splits[6], part), 7)
    hidden_states = centred(part_keys[0], (TOKENS, D), 1.0, 6.0, ((0, 16), (1, 2)))
    norm_gain = jnp.clip(1.0 + 0.18 * jax.random.normal(splits[1], (D,), jnp.float32), 0.099609375, 1.8984375).astype(jnp.bfloat16)
    up_proj = centred(splits[2], (EXPERTS, D, FFH), D ** -0.5, 0.09375, ((0, 16), (1, 2)))
    down_proj = centred(splits[3], (EXPERTS, FFH, D), FFH ** -0.5, 0.21875, ((0, 16), (2, 2)))
    expert_ids_keys = jax.random.split(jax.random.fold_in(part_keys[4], 1), TOKENS // TOK_DEV)
    expert_ids_turns = jax.random.permutation(jax.random.fold_in(part_keys[4], 3), TOKENS // TOK_DEV)
    expert_ids = jax.vmap(lambda own, number: deal_out(jax.random.fold_in(part_keys[4], 2), own, number, TOK_DEV, EXPERTS, TOPK, CAP, 2))(expert_ids_keys, expert_ids_turns).reshape((TOKENS, TOPK))
    combine_num = with_ends(jax.random.randint(part_keys[5], (TOKENS, TOPK), 2048, 65536), jax.random.fold_in(part_keys[5], 1), 2048, 65535).astype(jnp.int32)
    return {"hidden_states": hidden_states, "norm_gain": norm_gain, "up_proj": up_proj, "down_proj": down_proj, "expert_ids": expert_ids, "combine_num": combine_num}


def reference(hidden_states, norm_gain, up_proj, down_proj, expert_ids, combine_num):
    widened = hidden_states.astype(jnp.float32)
    mean_sq = lax.optimization_barrier(jnp.mean(widened * widened, axis=-1, keepdims=True))
    normed = (widened * lax.rsqrt(mean_sq + 1e-06) * norm_gain.astype(jnp.float32)).astype(jnp.bfloat16)
    flat_expert = expert_ids.reshape(-1).astype(jnp.int32)
    slot_total = flat_expert.shape[0]
    flat_token = (jnp.arange(slot_total, dtype=jnp.int32) // TOPK).astype(jnp.int32)
    flat_weight = combine_num.reshape(-1).astype(jnp.float32) / 65536.0
    order = jnp.argsort(flat_expert, stable=True).astype(jnp.int32)
    counts = lax.optimization_barrier(jnp.sum((flat_expert[:, None] == jnp.arange(EXPERTS, dtype=jnp.int32)[None, :]).astype(jnp.int32), axis=0))
    starts = (jnp.cumsum(counts) - counts).astype(jnp.int32)
    expert_rows = CAP * (TOKENS // TOK_DEV)
    padded_order = jnp.concatenate([order, jnp.zeros((expert_rows,), jnp.int32)])

    def per_expert(running, inputs):
        expert, up_matrix, down_matrix = inputs
        picked = lax.dynamic_slice_in_dim(padded_order, starts[expert], expert_rows)
        valid = jnp.arange(expert_rows, dtype=jnp.int32) < counts[expert]
        row_tokens = flat_token[picked]
        gathered_rows = normed[row_tokens]
        hidden = jax.nn.silu(jnp.dot(gathered_rows, up_matrix, preferred_element_type=jnp.float32)).astype(jnp.bfloat16)
        expert_out = jnp.dot(hidden, down_matrix, preferred_element_type=jnp.float32).astype(jnp.bfloat16)
        factor = jnp.where(valid, flat_weight[picked], jnp.zeros_like(flat_weight[picked]))
        running = running.at[row_tokens].add(factor[:, None] * expert_out.astype(jnp.float32))
        return (running, None)
    initial = jnp.zeros((hidden_states.shape[0], hidden_states.shape[1]), jnp.float32)
    running, _ = lax.scan(per_expert, initial, (jnp.arange(EXPERTS, dtype=jnp.int32), up_proj, down_proj))
    return running.astype(jnp.bfloat16)
```

```python
import functools

import jax
import jax.numpy as jnp
from jax import lax
from jax.experimental import pallas as pl
from jax.experimental.pallas import tpu as pltpu
from jax.sharding import PartitionSpec as P

D = 4096
EPS = 1e-06
YS = 2
F32 = jnp.float32
BF16 = jnp.bfloat16


def routed_body(hidden_states, norm_gain, up_proj, down_proj, expert_ids, combine_num):
    token_count, local_width = hidden_states.shape
    top_count = expert_ids.shape[1]
    ep_count = lax.axis_size("ep")
    sp_count = lax.axis_size("sp")
    expert_count = ep_count * sp_count
    routed = token_count * top_count
    capacity = max(2, min(token_count, routed // expert_count + routed // (4 * expert_count)))
    slot_count = expert_count * capacity
    widened = hidden_states.astype(F32)
    square_part = jnp.sum(widened * widened, axis=-1)
    square_total = lax.psum(square_part, "dp")
    mean_sq = (square_total / D)[:, None]
    normed = (widened * lax.rsqrt(mean_sq + EPS) * norm_gain.astype(F32)).astype(BF16)
    flat_expert = expert_ids.reshape(-1)
    onehot = (flat_expert[:, None] == jnp.arange(expert_count, dtype=jnp.int32)[None, :]).astype(
        jnp.int32
    )
    before = jnp.cumsum(onehot, axis=0) - onehot
    position = jnp.sum(before * onehot, axis=1)
    target = flat_expert * capacity + position
    placed = (jnp.arange(slot_count, dtype=jnp.int32)[:, None] == target[None, :]).astype(F32)
    select = placed.reshape(slot_count, token_count, top_count).sum(axis=2)
    outgoing = jnp.dot(select.astype(BF16), normed, preferred_element_type=F32)
    outgoing = outgoing.astype(BF16).reshape(expert_count, capacity, local_width)
    weights = combine_num.reshape(-1).astype(F32) / 65536.0
    mixing = (placed * weights[None, :]).reshape(slot_count, token_count, top_count).sum(axis=2)
    mixing_high = mixing.astype(BF16)
    mixing_low = (mixing - mixing_high.astype(F32)).astype(BF16)
    incoming = lax.all_to_all(outgoing, ("ep", "sp"), split_axis=0, concat_axis=0, tiled=True)
    arriving = incoming.reshape(slot_count, local_width)
    partial_value = jnp.dot(arriving, up_proj[0], preferred_element_type=F32)
    summed = lax.psum(partial_value, "dp")
    hidden = jax.nn.silu(summed).astype(BF16)
    produced = jnp.dot(hidden, down_proj[0], preferred_element_type=F32).astype(BF16)
    leaving = produced.reshape(expert_count, capacity, local_width)
    returned = lax.all_to_all(leaving, ("ep", "sp"), split_axis=0, concat_axis=0, tiled=True)
    back_rows = returned.reshape(slot_count, local_width)
    mixed = jnp.einsum("st,sd->td", mixing_high, back_rows, preferred_element_type=F32)
    mixed = mixed + jnp.einsum("st,sd->td", mixing_low, back_rows, preferred_element_type=F32)
    return mixed.astype(BF16)


def kernel(cap, nz, h_hbm, g_ref, u_hbm, d_hbm, ids_ref, num_ref, out_ref,
           xg, sg, u_ref, d_ref, cbuf, pown, psend, precv, sqs, sqp, w8, rk8, selb, wcol, rcol,
           hid, yb, crecv, yrecv, zb, za,
           lsem, agr, su, sd, sy, sc, ss, sr, xs, xr, qs, qr, cs, cr, ys, yr, zs_s, zbr, zar):
    toks, width = h_hbm.shape
    ff = u_hbm.shape[2]
    top = ids_ref.shape[1]
    ep, c, x = lax.axis_index("ep"), lax.axis_index("sp"), lax.axis_index("dp")
    z, y = lax.div(ep, YS), lax.rem(ep, YS)
    me, oth = y * 2 + c, (1 - y) * 2 + c
    mec, othc = y * 2 + 1 - c, (1 - y) * 2 + 1 - c
    expert = ep * 2 + c
    up_dev, dn_dev = {"ep": ep + YS}, {"ep": ep - YS}
    y_dev, c_dev, x_dev = {"ep": ep + 1 - 2 * y}, {"sp": 1 - c}, {"dp": 1 - x}

    def rc(src, dst, ssem, rsem, dev):
        return pltpu.make_async_remote_copy(
            src_ref=src, dst_ref=dst, send_sem=ssem, recv_sem=rsem,
            device_id=dev, device_id_type=pl.DeviceIdType.MESH)

    def z_dev(d):
        return {"ep": lax.rem(z + d, nz) * YS + y}

    load_h = pltpu.make_async_copy(h_hbm, xg.at[z, me], lsem.at[0])
    load_u = pltpu.make_async_copy(u_hbm.at[0], u_ref, lsem.at[1])
    load_d = pltpu.make_async_copy(d_hbm.at[0], d_ref, lsem.at[2])
    load_h.start()
    load_u.start()
    load_d.start()

    barrier = pltpu.get_barrier_semaphore()
    partners = [y_dev, c_dev, x_dev] + [z_dev(d) for d in range(1, nz)]
    for dev in partners:
        pl.semaphore_signal(barrier, inc=1, device_id=dev, device_id_type=pl.DeviceIdType.MESH)
    pl.semaphore_wait(barrier, len(partners))

    def z_up(zs):
        return rc(xg.at[zs, me], xg.at[zs, me], su.at[zs], agr.at[zs, me], up_dev)

    def z_dn(zs):
        return rc(xg.at[zs, me], xg.at[zs, me], sd.at[zs], agr.at[zs, me], dn_dev)

    def to_y(zs):
        return rc(xg.at[zs, me], xg.at[zs, me], sy.at[zs], agr.at[zs, me], y_dev)

    def to_c(zs, which):
        slot = me if which == 0 else oth
        return rc(xg.at[zs, slot], xg.at[zs, slot], sc.at[zs, which], agr.at[zs, slot], c_dev)

    def arrived(zs, slot):
        rc(xg.at[zs, slot], xg.at[zs, slot], sc.at[zs, 0], agr.at[zs, slot], c_dev).wait_recv()

    load_h.wait()

    @pl.when(z < nz - 1)
    def _():
        z_up(z).start()

    @pl.when(z > 0)
    def _():
        z_dn(z).start()

    lane = lax.broadcasted_iota(jnp.int32, (toks, 128), 1)
    hv = xg[z, me].astype(F32)
    acc = jnp.where(lane == 16, jnp.sum(hv * hv, axis=1, keepdims=True), 0.0)
    for k in range(top):
        wk = num_ref[:, k:k + 1].astype(F32) * (1.0 / 65536.0)
        acc = acc + jnp.where(lane == ids_ref[:, k:k + 1], wk, 0.0)
    sg[z, me] = acc.T[:24]
    st_c = rc(sg.at[z, me], sg.at[z, me], ss.at[0], sr.at[nz], c_dev)
    st_c.start()
    to_c(z, 0).start()
    st_c.wait_recv()
    pair = pl.ds(y * 2, 2)
    st_y = rc(sg.at[z, pair], sg.at[z, pair], ss.at[1], sr.at[nz + 1], y_dev)
    st_y.start()
    to_y(z).start()
    st_y.wait_recv()
    st_z = [rc(sg.at[z], sg.at[z], ss.at[1 + d], sr.at[z], z_dev(d)) for d in range(1, nz)]
    for cp in st_z:
        cp.start()

    def hop(h):
        @pl.when(z >= h)
        def _():
            zs = z - h
            arrived(zs, me)

            @pl.when(z < nz - 1)
            def _():
                z_up(zs).start()
            to_y(zs).start()
            to_c(zs, 0).start()

        @pl.when(z + h < nz)
        def _():
            zs = z + h
            arrived(zs, me)

            @pl.when(z > 0)
            def _():
                z_dn(zs).start()
            to_y(zs).start()
            to_c(zs, 0).start()

    low = z < 2
    order = [z, z + 1 - 2 * lax.rem(z, 2), jnp.where(low, 2, 1), jnp.where(low, 3, 0)]
    tri = (lax.broadcasted_iota(jnp.int32, (toks, toks), 0)
           < lax.broadcasted_iota(jnp.int32, (toks, toks), 1)).astype(BF16)
    spot = lax.broadcasted_iota(jnp.int32, (cap, toks), 0)

    def x_copy(k):
        return rc(psend.at[k], precv.at[k], xs.at[k], xr.at[k], x_dev)

    def q_copy(k):
        return rc(sqs.at[k], sqp.at[k], qs.at[k], qr.at[k], x_dev)

    def first(k):
        zs = order[k]
        if k > 0:
            rc(sg.at[zs], sg.at[zs], ss.at[2], sr.at[zs], c_dev).wait_recv()
        for s in range(4):
            w8[k, s:s + 1] = sg[zs, s, pl.ds(expert, 1), :]
            sqs[k, s:s + 1] = sg[zs, s, 16:17, :]
            w8[k, 4 + s:5 + s] = jnp.zeros((1, toks), F32)
            sqs[k, 4 + s:5 + s] = jnp.zeros((1, toks), F32)
        q_copy(k).start()
        named = w8[k] > 0.0
        rank = jnp.dot(named.astype(F32).astype(BF16), tri, preferred_element_type=F32)
        rk8[k] = jnp.where(named, rank.astype(jnp.int32), -1)
        for s in range(4):
            sel = spot == rk8[k, s:s + 1]
            selb[k, s * cap:(s + 1) * cap] = sel.astype(F32).astype(BF16)
            wcol[k, s * cap:(s + 1) * cap] = jnp.sum(
                jnp.where(sel, w8[k, s:s + 1], 0.0), axis=1, keepdims=True)
        arrived(zs, oth)
        to_c(zs, 1).start()
        arrived(zs, mec)
        arrived(zs, othc)

        @pl.loop(0, width // 512)
        def _(t):
            cols = pl.ds(pl.multiple_of(t * 512, 512), 512)
            gain = g_ref[:, cols].astype(F32)
            for s in range(4):
                rows = slice(s * cap, (s + 1) * cap)
                picked = jnp.dot(selb[k, rows], xg[zs, s, :, cols], preferred_element_type=F32)
                cbuf[rows, cols] = (picked * gain).astype(BF16)

        if k == 0:
            load_u.wait()

        @pl.loop(0, ff // 256)
        def _(t):
            cols = pl.ds(pl.multiple_of(t * 256, 256), 256)
            part = jnp.dot(cbuf[...], u_ref[:, cols], preferred_element_type=F32)
            pown[k, :, cols] = part
            psend[k, :, cols] = part.astype(BF16)
        x_copy(k).start()

    for k in range(nz):
        if k < nz - 1:
            hop(k + 1)
        first(k)

    def core_copy(k, yy):
        return rc(yb.at[k, yy * 2 + 1 - c], crecv.at[k, yy], cs.at[k, yy], cr.at[k, yy], c_dev)

    def core_arrived(k, yy):
        rc(yb.at[k, me], crecv.at[k, yy], cs.at[k, 0], cr.at[k, yy], c_dev).wait_recv()

    def y_copy(k):
        return rc(yb.at[k, oth], yrecv.at[k], ys.at[k], yr.at[k], y_dev)

    def up_copy(k, zs):
        return rc(yb.at[k, me], zb.at[zs], zs_s.at[k], zbr.at[zs], up_dev)

    def dn_copy(k, zs):
        return rc(yb.at[k, me], za.at[zs], zs_s.at[k], zar.at[zs], dn_dev)

    def second(k):
        q_copy(k).wait_recv()
        scale = lax.rsqrt((sqs[k] + sqp[k]) * (1.0 / D) + EPS)
        for s in range(4):
            sel = spot == rk8[k, s:s + 1]
            rcol[s * cap:(s + 1) * cap] = jnp.sum(
                jnp.where(sel, scale[s:s + 1], 0.0), axis=1, keepdims=True)
        x_copy(k).wait_recv()

        @pl.loop(0, ff // 256)
        def _(t):
            cols = pl.ds(pl.multiple_of(t * 256, 256), 256)
            v = (pown[k, :, cols] + precv[k, :, cols].astype(F32)) * rcol[...]
            hid[:, cols] = (v / (1.0 + jnp.exp(-v))).astype(BF16)

        @pl.loop(0, width // 512)
        def _(t):
            cols = pl.ds(pl.multiple_of(t * 512, 512), 512)
            made = jnp.dot(hid[...], d_ref[:, cols], preferred_element_type=F32)
            made = (made * wcol[k]).astype(BF16)
            for s in range(4):
                rows = slice(s * cap, (s + 1) * cap)
                yb[k, s, :, cols] = lax.dot_general(
                    selb[k, rows], made[rows], (((0,), (0,)), ((), ())),
                    preferred_element_type=F32).astype(BF16)
        core_copy(k, 1 - y).start()
        core_copy(k, y).start()

    def across(k):
        core_arrived(k, 1 - y)
        yb[k, oth] = (yb[k, oth].astype(F32) + crecv[k, 1 - y].astype(F32)).astype(BF16)
        y_copy(k).start()

    def along(k):
        zs = order[k]
        core_arrived(k, y)
        y_copy(k).wait_recv()
        total = yb[k, me].astype(F32) + crecv[k, y].astype(F32) + yrecv[k].astype(F32)
        if k == 0:
            out_ref[...] = total.astype(BF16)

            @pl.when((z > 0) & (z < nz - 1))
            def _():
                up_copy(k, zs).wait_recv()
                dn_copy(k, zs).wait_recv()
                out_ref[...] = (total + zb[zs].astype(F32) + za[zs].astype(F32)).astype(BF16)

            @pl.when(z == 0)
            def _():
                dn_copy(k, zs).wait_recv()
                out_ref[...] = (total + za[zs].astype(F32)).astype(BF16)

            @pl.when(z == nz - 1)
            def _():
                up_copy(k, zs).wait_recv()
                out_ref[...] = (total + zb[zs].astype(F32)).astype(BF16)
        else:
            yb[k, me] = total.astype(BF16)

            @pl.when((zs > z) & (z > 0))
            def _():
                up_copy(k, zs).wait_recv()
                yb[k, me] = (total + zb[zs].astype(F32)).astype(BF16)

            @pl.when((zs < z) & (z < nz - 1))
            def _():
                dn_copy(k, zs).wait_recv()
                yb[k, me] = (total + za[zs].astype(F32)).astype(BF16)

            @pl.when(zs > z)
            def _():
                up_copy(k, zs).start()

            @pl.when(zs < z)
            def _():
                dn_copy(k, zs).start()

    load_d.wait()
    second(2)
    across(2)
    second(3)
    across(3)
    along(2)
    second(1)
    across(1)
    along(3)
    second(0)
    across(0)
    along(1)
    along(0)

    for zs in range(nz):
        @pl.when((zs <= z) & (z < nz - 1))
        def _():
            z_up(zs).wait_send()

        @pl.when((zs >= z) & (z > 0))
        def _():
            z_dn(zs).wait_send()
        to_y(zs).wait_send()
        to_c(zs, 0).wait_send()
        to_c(zs, 1).wait_send()
    st_c.wait_send()
    st_y.wait_send()
    for cp in st_z:
        cp.wait_send()
    for k in range(nz):
        x_copy(k).wait_send()
        q_copy(k).wait_send()
        core_copy(k, y).wait_send()
        core_copy(k, 1 - y).wait_send()
        y_copy(k).wait_send()
        if k > 0:
            up_copy(k, order[k]).wait_send()


def dense_body(hidden_states, norm_gain, up_proj, down_proj, expert_ids, combine_num):
    toks, width = hidden_states.shape
    top = expert_ids.shape[1]
    ff = up_proj.shape[2]
    nz = lax.axis_size("ep") // YS
    experts = lax.axis_size("ep") * lax.axis_size("sp")
    routed = toks * top
    cap = min(toks, routed // experts + routed // (4 * experts))
    rows = 4 * cap
    dma = pltpu.SemaphoreType.DMA
    vmem = pl.BlockSpec(memory_space=pltpu.VMEM)
    hbm = pl.BlockSpec(memory_space=pl.ANY)
    return pl.pallas_call(
        functools.partial(kernel, cap, nz),
        out_shape=jax.ShapeDtypeStruct((toks, width), BF16),
        in_specs=[hbm, vmem, hbm, hbm, vmem, vmem],
        out_specs=vmem,
        scratch_shapes=[
            pltpu.VMEM((nz, 4, toks, width), BF16),
            pltpu.VMEM((nz, 4, 24, toks), F32),
            pltpu.VMEM((width, ff), BF16),
            pltpu.VMEM((ff, width), BF16),
            pltpu.VMEM((rows, width), BF16),
            pltpu.VMEM((nz, rows, ff), F32),
            pltpu.VMEM((nz, rows, ff), BF16),
            pltpu.VMEM((nz, rows, ff), BF16),
            pltpu.VMEM((nz, 8, toks), F32),
            pltpu.VMEM((nz, 8, toks), F32),
            pltpu.VMEM((nz, 8, toks), F32),
            pltpu.VMEM((nz, 8, toks), jnp.int32),
            pltpu.VMEM((nz, rows, toks), BF16),
            pltpu.VMEM((nz, rows, 1), F32),
            pltpu.VMEM((rows, 1), F32),
            pltpu.VMEM((rows, ff), BF16),
            pltpu.VMEM((nz, 4, toks, width), BF16),
            pltpu.VMEM((nz, 2, toks, width), BF16),
            pltpu.VMEM((nz, toks, width), BF16),
            pltpu.VMEM((nz, toks, width), BF16),
            pltpu.VMEM((nz, toks, width), BF16),
            dma((3,)), dma((nz, 4)), dma((nz,)), dma((nz,)), dma((nz,)), dma((nz, 2)),
            dma((nz + 1,)), dma((nz + 2,)), dma((nz,)), dma((nz,)), dma((nz,)), dma((nz,)),
            dma((nz, 2)), dma((nz, 2)), dma((nz,)), dma((nz,)), dma((nz,)), dma((nz,)), dma((nz,)),
        ],
        compiler_params=pltpu.CompilerParams(
            collective_id=0, has_side_effects=True, vmem_limit_bytes=58 * 1024 * 1024),
        cost_estimate=pl.CostEstimate(
            flops=4 * 4 * rows * width * ff, bytes_accessed=4 * width * ff, transcendentals=0),
    )(hidden_states, norm_gain.reshape(1, width), up_proj, down_proj, expert_ids, combine_num)


def solution(mesh):
    spec = (
        P(("rep", "ep", "sp"), "dp"),
        P("dp"),
        P(("ep", "sp"), "dp", None),
        P(("ep", "sp"), None, "dp"),
        P(("rep", "ep", "sp"), None),
        P(("rep", "ep", "sp"), None),
    )
    sizes = dict(mesh.shape)
    dense = (sizes["rep"], sizes["ep"], sizes["dp"], sizes["sp"]) == (1, 8, 2, 2)
    return jax.shard_map(
        dense_body if dense else routed_body,
        mesh=mesh, in_specs=spec, out_specs=P(("rep", "ep", "sp"), "dp"), check_vma=False
    )
```

```python
import functools

import jax
import jax.numpy as jnp
from jax import lax
from jax.experimental import pallas as pl
from jax.experimental.pallas import tpu as pltpu
from jax.sharding import PartitionSpec as P

D = 4096
EPS = 1e-06
IN_PARTS = 2
BACK_PARTS = 4
YS = 2
F32 = jnp.float32
BF16 = jnp.bfloat16


def routed_body(hidden_states, norm_gain, up_proj, down_proj, expert_ids, combine_num):
    token_count, local_width = hidden_states.shape
    top_count = expert_ids.shape[1]
    ep_count = lax.axis_size("ep")
    sp_count = lax.axis_size("sp")
    expert_count = ep_count * sp_count
    routed = token_count * top_count
    capacity = max(2, min(token_count, routed // expert_count + routed // (4 * expert_count)))
    slot_count = expert_count * capacity
    widened = hidden_states.astype(F32)
    square_part = jnp.sum(widened * widened, axis=-1)
    square_total = lax.psum(square_part, "dp")
    mean_sq = (square_total / D)[:, None]
    normed = (widened * lax.rsqrt(mean_sq + EPS) * norm_gain.astype(F32)).astype(BF16)
    flat_expert = expert_ids.reshape(-1)
    onehot = (flat_expert[:, None] == jnp.arange(expert_count, dtype=jnp.int32)[None, :]).astype(
        jnp.int32
    )
    before = jnp.cumsum(onehot, axis=0) - onehot
    position = jnp.sum(before * onehot, axis=1)
    target = flat_expert * capacity + position
    placed = (jnp.arange(slot_count, dtype=jnp.int32)[:, None] == target[None, :]).astype(F32)
    select = placed.reshape(slot_count, token_count, top_count).sum(axis=2)
    outgoing = jnp.dot(select.astype(BF16), normed, preferred_element_type=F32)
    outgoing = outgoing.astype(BF16).reshape(expert_count, capacity, local_width)
    weights = combine_num.reshape(-1).astype(F32) / 65536.0
    mixing = (placed * weights[None, :]).reshape(slot_count, token_count, top_count).sum(axis=2)
    mixing_high = mixing.astype(BF16)
    mixing_low = (mixing - mixing_high.astype(F32)).astype(BF16)
    incoming = lax.all_to_all(outgoing, ("ep", "sp"), split_axis=0, concat_axis=0, tiled=True)
    arriving = incoming.reshape(slot_count, local_width)
    partial_value = jnp.dot(arriving, up_proj[0], preferred_element_type=F32)
    summed = lax.psum(partial_value, "dp")
    hidden = jax.nn.silu(summed).astype(BF16)
    produced = jnp.dot(hidden, down_proj[0], preferred_element_type=F32).astype(BF16)
    leaving = produced.reshape(expert_count, capacity, local_width)
    returned = lax.all_to_all(leaving, ("ep", "sp"), split_axis=0, concat_axis=0, tiled=True)
    back_rows = returned.reshape(slot_count, local_width)
    mixed = jnp.einsum("st,sd->td", mixing_high, back_rows, preferred_element_type=F32)
    mixed = mixed + jnp.einsum("st,sd->td", mixing_low, back_rows, preferred_element_type=F32)
    return mixed.astype(BF16)


def kernel(cap, nz, h_hbm, g_ref, u_hbm, d_hbm, ids_ref, num_ref, out_ref,
           xg, sg, u_ref, d_ref, cbuf, pown, psend, precv, sqs, sqp, w8, rk8, selb, wcol, rcol,
           hid, yb, crecv, yrecv, zb, za, gs,
           lsem, agr, su, sd, sy, sc, ss, sr, xs, xr, qs, qr, cs, cr, ys, yr, zs_s, zbr, zar):
    toks, width = h_hbm.shape
    ff = u_hbm.shape[2]
    top = ids_ref.shape[0]
    step_in, step_back = width // IN_PARTS, width // BACK_PARTS
    parts_in = [pl.ds(i * step_in, step_in) for i in range(IN_PARTS)]
    parts_back = [pl.ds(i * step_back, step_back) for i in range(BACK_PARTS)]
    ep, c, x = lax.axis_index("ep"), lax.axis_index("sp"), lax.axis_index("dp")
    z, y = lax.div(ep, YS), lax.rem(ep, YS)
    me, oth = y * 2 + c, (1 - y) * 2 + c
    mec, othc = y * 2 + 1 - c, (1 - y) * 2 + 1 - c
    expert = ep * 2 + c
    up_dev, dn_dev = {"ep": ep + YS}, {"ep": ep - YS}
    y_dev, c_dev, x_dev = {"ep": ep + 1 - 2 * y}, {"sp": 1 - c}, {"dp": 1 - x}

    def rc(src, dst, ssem, rsem, dev):
        return pltpu.make_async_remote_copy(
            src_ref=src, dst_ref=dst, send_sem=ssem, recv_sem=rsem,
            device_id=dev, device_id_type=pl.DeviceIdType.MESH)

    def z_dev(d):
        return {"ep": lax.rem(z + d, nz) * YS + y}

    load_h = pltpu.make_async_copy(h_hbm, xg.at[z, me], lsem.at[0])
    load_u = pltpu.make_async_copy(u_hbm.at[0], u_ref, lsem.at[1])
    load_d = pltpu.make_async_copy(d_hbm.at[0], d_ref, lsem.at[2])
    load_h.start()
    load_u.start()
    load_d.start()

    barrier = pltpu.get_barrier_semaphore()
    partners = [y_dev, c_dev, x_dev] + [z_dev(d) for d in range(1, nz)]
    for dev in partners:
        pl.semaphore_signal(barrier, inc=1, device_id=dev, device_id_type=pl.DeviceIdType.MESH)
    pl.semaphore_wait(barrier, len(partners))

    def z_up(zs, i):
        ref = xg.at[zs, me, :, parts_in[i]]
        return rc(ref, ref, su.at[zs, i], agr.at[zs, me, i], up_dev)

    def z_dn(zs, i):
        ref = xg.at[zs, me, :, parts_in[i]]
        return rc(ref, ref, sd.at[zs, i], agr.at[zs, me, i], dn_dev)

    def to_y(zs, i):
        ref = xg.at[zs, me, :, parts_in[i]]
        return rc(ref, ref, sy.at[zs, i], agr.at[zs, me, i], y_dev)

    def from_y(zs, i):
        ref = xg.at[zs, oth, :, parts_in[i]]
        rc(ref, ref, sy.at[zs, i], agr.at[zs, oth, i], y_dev).wait_recv()

    def to_c(zs, which):
        slot = me if which == 0 else oth
        return rc(xg.at[zs, slot], xg.at[zs, slot], sc.at[zs, which], agr.at[zs, slot, 0], c_dev)

    def arrived(zs, slot):
        rc(xg.at[zs, slot], xg.at[zs, slot], sc.at[zs, 0], agr.at[zs, slot, 0], c_dev).wait_recv()

    load_h.wait()

    for i in range(IN_PARTS):
        @pl.when(z < nz - 1)
        def _():
            z_up(z, i).start()

        @pl.when(z > 0)
        def _():
            z_dn(z, i).start()

    row = lax.broadcasted_iota(jnp.int32, (24, toks), 0)
    hv = xg[z, me].astype(F32)
    squares = jnp.broadcast_to(jnp.sum(hv * hv, axis=1, keepdims=True), (toks, 128)).T
    acc = jnp.where(row == 16, squares[:24], 0.0)
    for k in range(top):
        wk = num_ref[k:k + 1].astype(F32) * (1.0 / 65536.0)
        acc = acc + jnp.where(row == ids_ref[k:k + 1], wk, 0.0)
    sg[z, me] = acc
    st_c = rc(sg.at[z, me], sg.at[z, me], ss.at[0], sr.at[nz], c_dev)
    st_c.start()
    to_c(z, 0).start()
    st_c.wait_recv()
    pair = pl.ds(y * 2, 2)
    st_y = rc(sg.at[z, pair], sg.at[z, pair], ss.at[1], sr.at[nz + 1], y_dev)
    st_y.start()
    for i in range(IN_PARTS):
        to_y(z, i).start()
    st_y.wait_recv()
    st_z = [rc(sg.at[z], sg.at[z], ss.at[1 + d], sr.at[z], z_dev(d)) for d in range(1, nz)]
    for cp in st_z:
        cp.start()

    def hop(h):
        for i in range(IN_PARTS):
            @pl.when(z >= h)
            def _():
                z_up(z - h, i).wait_recv()

                @pl.when(z < nz - 1)
                def _():
                    z_up(z - h, i).start()
                to_y(z - h, i).start()

            @pl.when(z + h < nz)
            def _():
                z_dn(z + h, i).wait_recv()

                @pl.when(z > 0)
                def _():
                    z_dn(z + h, i).start()
                to_y(z + h, i).start()

        @pl.when(z >= h)
        def _():
            to_c(z - h, 0).start()

        @pl.when(z + h < nz)
        def _():
            to_c(z + h, 0).start()

    gs[...] = g_ref[...].astype(F32).reshape(1, width)
    inner = (z > 0) & (z < nz - 1)
    order = [z, 1 + lax.rem(z, 2),
             jnp.where(z == 0, 2, jnp.where(z == 1, 0, jnp.where(z == 2, 3, 1))),
             jnp.where(z < 2, 3, 0)]
    tri = (lax.broadcasted_iota(jnp.int32, (toks, toks), 0)
           < lax.broadcasted_iota(jnp.int32, (toks, toks), 1)).astype(BF16)
    spot = lax.broadcasted_iota(jnp.int32, (cap, toks), 0)

    def half_rows(yy):
        return pl.ds(pl.multiple_of(yy * 2 * cap, 16), 2 * cap)

    def x_copy(k, yy):
        rows = half_rows(yy)
        return rc(psend.at[k, rows], precv.at[k, rows], xs.at[k, yy], xr.at[k, yy], x_dev)

    def q_copy(k):
        return rc(sqs.at[k], sqp.at[k], qs.at[k], qr.at[k], x_dev)

    def first(k):
        zs = order[k]
        if k > 0:
            rc(sg.at[zs], sg.at[zs], ss.at[2], sr.at[zs], c_dev).wait_recv()
        for s in range(4):
            w8[k, s:s + 1] = sg[zs, s, pl.ds(expert, 1), :]
            sqs[k, s:s + 1] = sg[zs, s, 16:17, :]
            w8[k, 4 + s:5 + s] = jnp.zeros((1, toks), F32)
            sqs[k, 4 + s:5 + s] = jnp.zeros((1, toks), F32)
        q_copy(k).start()
        named = w8[k] > 0.0
        rank = jnp.dot(named.astype(F32).astype(BF16), tri, preferred_element_type=F32)
        rk8[k] = jnp.where(named, rank.astype(jnp.int32), -1)
        for s in range(4):
            sel = spot == rk8[k, s:s + 1]
            selb[k, s * cap:(s + 1) * cap] = sel.astype(F32).astype(BF16)
            wcol[k, s * cap:(s + 1) * cap] = jnp.sum(
                jnp.where(sel, w8[k, s:s + 1], 0.0), axis=1, keepdims=True)
        arrived(zs, mec)
        up_half(k, zs, y)
        for i in range(IN_PARTS):
            from_y(zs, i)
        to_c(zs, 1).start()
        arrived(zs, othc)
        up_half(k, zs, 1 - y)

    def up_half(k, zs, yy):
        @pl.loop(0, width // 512)
        def _(t):
            cols = pl.ds(pl.multiple_of(t * 512, 512), 512)
            for j in range(2):
                s = yy * 2 + j
                rows = pl.ds(pl.multiple_of(s * cap, 16), cap)
                picked = jnp.dot(selb[k, rows], xg[zs, s, :, cols], preferred_element_type=F32)
                cbuf[j * cap:(j + 1) * cap, cols] = (picked * gs[:, cols]).astype(BF16)

        half = half_rows(yy)

        @pl.loop(0, ff // 256)
        def _(t):
            cols = pl.ds(pl.multiple_of(t * 256, 256), 256)
            part = jnp.dot(cbuf[...], u_ref[:, cols], preferred_element_type=F32)
            pown[k, half, cols] = part
            psend[k, half, cols] = part.astype(BF16)
        x_copy(k, yy).start()

    load_u.wait()
    def core_copy(k, yy, i):
        cols = parts_back[i]
        return rc(yb.at[k, yy * 2 + 1 - c, :, cols], crecv.at[k, yy, :, cols],
                  cs.at[k, yy, i], cr.at[k, yy, i], c_dev)

    def y_copy(k, i):
        cols = parts_back[i]
        return rc(yb.at[k, oth, :, cols], yrecv.at[k, :, cols], ys.at[k, i], yr.at[k, i], y_dev)

    def up_copy(k, zs, i):
        cols = parts_back[i]
        return rc(yb.at[k, me, :, cols], zb.at[zs, :, cols], zs_s.at[k, i], zbr.at[zs, i], up_dev)

    def dn_copy(k, zs, i):
        cols = parts_back[i]
        return rc(yb.at[k, me, :, cols], za.at[zs, :, cols], zs_s.at[k, i], zar.at[zs, i], dn_dev)

    def second(k):
        q_copy(k).wait_recv()
        scale = lax.rsqrt((sqs[k] + sqp[k]) * (1.0 / D) + EPS)
        for s in range(4):
            sel = spot == rk8[k, s:s + 1]
            rcol[s * cap:(s + 1) * cap] = jnp.sum(
                jnp.where(sel, scale[s:s + 1], 0.0), axis=1, keepdims=True)
        x_copy(k, y).wait_recv()
        x_copy(k, 1 - y).wait_recv()

        @pl.loop(0, ff // 256)
        def _(t):
            cols = pl.ds(pl.multiple_of(t * 256, 256), 256)
            v = (pown[k, :, cols] + precv[k, :, cols].astype(F32)) * rcol[...]
            hid[:, cols] = (v / (1.0 + jnp.exp(-v))).astype(BF16)

        def produce(cols):
            made = jnp.dot(hid[...], d_ref[:, cols], preferred_element_type=F32)
            made = (made * wcol[k]).astype(BF16)
            for s in range(4):
                rows = slice(s * cap, (s + 1) * cap)
                yb[k, s, :, cols] = lax.dot_general(
                    selb[k, rows], made[rows], (((0,), (0,)), ((), ())),
                    preferred_element_type=F32).astype(BF16)

        for i in range(BACK_PARTS):
            @pl.loop(0, step_back // 512)
            def _(t):
                produce(pl.ds(pl.multiple_of(i * step_back + t * 512, 512), 512))
            core_copy(k, 1 - y, i).start()
            core_copy(k, y, i).start()

    def across(k):
        for i, cols in enumerate(parts_back):
            core_copy(k, 1 - y, i).wait_recv()
            yb[k, oth, :, cols] = (yb[k, oth, :, cols].astype(F32)
                                   + crecv[k, 1 - y, :, cols].astype(F32)).astype(BF16)
            y_copy(k, i).start()

    def along(k, zs, last=False):
        for i, cols in enumerate(parts_back):
            core_copy(k, y, i).wait_recv()
            y_copy(k, i).wait_recv()

            def add(chains):
                total = (yb[k, me, :, cols].astype(F32) + crecv[k, y, :, cols].astype(F32)
                         + yrecv[k, :, cols].astype(F32))
                for copy, buf in chains:
                    copy(k, zs, i).wait_recv()
                    total = total + buf[zs, :, cols].astype(F32)
                if last:
                    out_ref[:, cols] = total.astype(BF16)
                else:
                    yb[k, me, :, cols] = total.astype(BF16)

            below, above = (up_copy, zb), (dn_copy, za)
            if last:
                pl.when(inner)(lambda: add([below, above]))
                pl.when(z == 0)(lambda: add([above]))
                pl.when(z == nz - 1)(lambda: add([below]))
            else:
                pl.when(inner & (zs > z))(lambda: add([below]))
                pl.when(inner & (zs < z))(lambda: add([above]))
                pl.when((z == 0) | (z == nz - 1))(lambda: add([]))

                @pl.when(zs > z)
                def _():
                    up_copy(k, zs, i).start()

                @pl.when(zs < z)
                def _():
                    dn_copy(k, zs, i).start()

    hop(1)
    first(0)
    hop(2)
    first(1)
    hop(3)
    first(2)
    load_d.wait()
    late = jnp.where(inner, 3, 2), jnp.where(inner, 2, 3)
    dest = jnp.where(inner, order[3], order[2]), jnp.where(inner, order[2], order[3])
    second(1)
    across(1)
    first(3)
    second(2)
    across(2)
    along(1, order[1])
    second(3)
    across(3)
    second(0)
    across(0)
    along(late[0], dest[0])
    along(late[1], dest[1])
    along(0, order[0], True)

    for zs in range(nz):
        for i in range(IN_PARTS):
            @pl.when((zs <= z) & (z < nz - 1))
            def _():
                z_up(zs, i).wait_send()

            @pl.when((zs >= z) & (z > 0))
            def _():
                z_dn(zs, i).wait_send()
            to_y(zs, i).wait_send()
        to_c(zs, 0).wait_send()
        to_c(zs, 1).wait_send()
    st_c.wait_send()
    st_y.wait_send()
    for cp in st_z:
        cp.wait_send()
    for k in range(nz):
        x_copy(k, y).wait_send()
        x_copy(k, 1 - y).wait_send()
        q_copy(k).wait_send()
        for i in range(BACK_PARTS):
            core_copy(k, y, i).wait_send()
            core_copy(k, 1 - y, i).wait_send()
            y_copy(k, i).wait_send()
            if k > 0:
                up_copy(k, order[k], i).wait_send()


def dense_body(hidden_states, norm_gain, up_proj, down_proj, expert_ids, combine_num):
    toks, width = hidden_states.shape
    top = expert_ids.shape[1]
    ff = up_proj.shape[2]
    nz = lax.axis_size("ep") // YS
    experts = lax.axis_size("ep") * lax.axis_size("sp")
    routed = toks * top
    cap = min(toks, routed // experts + routed // (4 * experts))
    rows = 4 * cap
    ni, nb = IN_PARTS, BACK_PARTS
    dma = pltpu.SemaphoreType.DMA
    vmem = pl.BlockSpec(memory_space=pltpu.VMEM)
    hbm = pl.BlockSpec(memory_space=pl.ANY)
    return pl.pallas_call(
        functools.partial(kernel, cap, nz),
        out_shape=jax.ShapeDtypeStruct((toks, width), BF16),
        in_specs=[hbm, vmem, hbm, hbm, vmem, vmem],
        out_specs=vmem,
        scratch_shapes=[
            pltpu.VMEM((nz, 4, toks, width), BF16),
            pltpu.VMEM((nz, 4, 24, toks), F32),
            pltpu.VMEM((width, ff), BF16),
            pltpu.VMEM((ff, width), BF16),
            pltpu.VMEM((2 * cap, width), BF16),
            pltpu.VMEM((nz, rows, ff), F32),
            pltpu.VMEM((nz, rows, ff), BF16),
            pltpu.VMEM((nz, rows, ff), BF16),
            pltpu.VMEM((nz, 8, toks), F32),
            pltpu.VMEM((nz, 8, toks), F32),
            pltpu.VMEM((nz, 8, toks), F32),
            pltpu.VMEM((nz, 8, toks), jnp.int32),
            pltpu.VMEM((nz, rows, toks), BF16),
            pltpu.VMEM((nz, rows, 1), F32),
            pltpu.VMEM((rows, 1), F32),
            pltpu.VMEM((rows, ff), BF16),
            pltpu.VMEM((nz, 4, toks, width), BF16),
            pltpu.VMEM((nz, 2, toks, width), BF16),
            pltpu.VMEM((nz, toks, width), BF16),
            pltpu.VMEM((nz, toks, width), BF16),
            pltpu.VMEM((nz, toks, width), BF16),
            pltpu.VMEM((1, width), F32),
            dma((3,)), dma((nz, 4, ni)), dma((nz, ni)), dma((nz, ni)), dma((nz, ni)), dma((nz, 2)),
            dma((nz + 1,)), dma((nz + 2,)), dma((nz, 2)), dma((nz, 2)), dma((nz,)), dma((nz,)),
            dma((nz, 2, nb)), dma((nz, 2, nb)), dma((nz, nb)), dma((nz, nb)), dma((nz, nb)),
            dma((nz, nb)), dma((nz, nb)),
        ],
        compiler_params=pltpu.CompilerParams(
            collective_id=0, has_side_effects=True, vmem_limit_bytes=58 * 1024 * 1024),
        cost_estimate=pl.CostEstimate(
            flops=4 * 4 * rows * width * ff, bytes_accessed=4 * width * ff, transcendentals=0),
    )(hidden_states, norm_gain, up_proj, down_proj, expert_ids.T, combine_num.T)


def solution(mesh):
    spec = (
        P(("rep", "ep", "sp"), "dp"),
        P("dp"),
        P(("ep", "sp"), "dp", None),
        P(("ep", "sp"), None, "dp"),
        P(("rep", "ep", "sp"), None),
        P(("rep", "ep", "sp"), None),
    )
    sizes = dict(mesh.shape)
    dense = (sizes["rep"], sizes["ep"], sizes["dp"], sizes["sp"]) == (1, 8, 2, 2)
    return jax.shard_map(
        dense_body if dense else routed_body,
        mesh=mesh, in_specs=spec, out_specs=P(("rep", "ep", "sp"), "dp"), check_vma=False
    )
```
